32 devices in a mesh: ep: 4 (over y, x), edp: 8 (over z, core).
Axes of the slice: x: 2, y: 2, z: 4, core: 2. Of those that a mesh axis runs over, the one named last changes fastest.
Arguments:
- tokens: bfloat16 [512, 4096], P('ep', 'edp'), may hold values from -6 to 6
- out_grad: bfloat16 [512, 4096], P('ep', 'edp'), may hold values from -1.5 to 1.5
- probs: float32 [512, 8], P('ep'), may hold values from 0.1 to 1
- expert_ids: int32 [512, 8], P('ep'), may hold values from 0 to 127, all different within a row; in each aligned block of 128 rows (0 to 127, 128 to 255, ...) at most 16 rows name the same one
- w_gate: bfloat16 [8, 4096, 1024], P('edp', 'ep'), may hold values from -0.09375 to 0.09375
- w_up: bfloat16 [8, 4096, 1024], P('edp', 'ep'), may hold values from -0.09375 to 0.09375
- w_down: bfloat16 [8, 1024, 4096], P('edp', None, 'ep'), may hold values from -0.1875 to 0.1875
Outputs:
- token_grad: bfloat16 [512, 4096], P('ep', 'edp')
- grad_gate: bfloat16 [8, 4096, 1024], P('edp', 'ep')
- grad_up: bfloat16 [8, 4096, 1024], P('edp', 'ep')
- grad_down: bfloat16 [8, 1024, 4096], P('edp', None, 'ep')
The draws below stay inside these ranges and needn't reach their ends.
Inputs may be any that keep to these rules, and one draw needn't show every extreme that they name: `expert_ids`: each row names 8 different experts; within each context block of 128 tokens no expert is named by more than 16 tokens, a bound that some block reaches.
All inputs are finite; a program needn't handle non-finite values.
Results may differ from the reference program's by a relative error of at most 0.0058.
Values may be sent and summed in bfloat16 or wider, within the bound.
A program may use at most 64 MiB of HBM per device.

```python
import math
import jax
import jax.numpy as jnp
import numpy as np
from jax import lax

D = 4096
EXPERTS = 128
TOP = 8
HID = 1024
TOK_CTX = 128
CAP = 16
TOKENS = 512
EWIN = 8


def levels(rng, shape, cuts, low, largest):
    def one(axis_at, parts):
        draws = jax.random.uniform(jax.random.fold_in(jax.random.fold_in(rng, 6), axis_at), (parts,), jnp.float32, low / len(cuts), largest / len(cuts))
        return jnp.repeat(jnp.exp(draws), shape[axis_at] // parts).reshape((-1,) + (1,) * (len(shape) - axis_at - 1))

    loudness = one(*cuts[0])
    for cut in cuts[1:]:
        loudness = loudness * one(*cut)
    return loudness


def shared_out(key, own, number, rows, number_of, top, bound, skew):
    order = jax.random.permutation(key, number_of)
    heavy_load, usual = load_shares(number_of, rows * top, bound, skew, True), load_shares(number_of, rows * top, bound, skew, False)
    places = jnp.arange(number_of)

    def named(tallies, offset_by):
        used = int((tallies > 0).sum())
        fixed = max(1, used // 4)
        shifted = fixed + (places - fixed + offset_by * (used - fixed)) % max(1, number_of - fixed)
        return jnp.zeros((number_of,), jnp.int32).at[order[jnp.where(places < fixed, places, shifted)]].set(jnp.asarray(tallies, jnp.int32))

    tallies = jnp.where(number % 4 == 0, named(heavy_load, number // 4), named(usual, number - number // 4 - 1))
    mixed = jax.random.permutation(jax.random.fold_in(own, 3), number_of)
    giver, sink = mixed[0:number_of // 2 * 2:2], mixed[1:number_of // 2 * 2:2]
    margin = jnp.minimum(tallies[giver] - 1, bound - tallies[sink]) // 2
    margin = jnp.where((giver == order[0]) | (sink == order[0]) | (tallies[sink] == 0), 0, jnp.maximum(margin, 0))
    shifted = jax.random.randint(jax.random.fold_in(own, 4), (number_of // 2,), 0, 1 << 20) % (margin + 1)
    tallies = tallies.at[giver].add(-shifted).at[sink].add(shifted)
    labels = jnp.searchsorted(jnp.cumsum(tallies), jnp.arange(rows * top), side="right").astype(jnp.int32)
    table = labels.reshape(top, rows).T
    table = table[jax.random.permutation(jax.random.fold_in(own, 1), rows)]
    offset_by = jax.random.randint(jax.random.fold_in(own, 2), (rows, 1), 0, top)
    return jnp.take_along_axis(table, (jnp.arange(top)[None, :] + offset_by) % top, axis=1)


def load_shares(amount, total, limit, skew, full):
    weights = [(1 << 20) // math.isqrt(rank ** skew) + 1 for rank in range(1, amount + 1)]
    largest = limit if full else min(limit, max(-(-total // amount), total * weights[0] // sum(weights)))
    least = 1 if total - largest >= amount - 1 else 0
    given, surplus = [largest] + [least] * (amount - 1), total - largest - least * (amount - 1)
    while surplus > 0:
        movable = [i for i in range(1, amount) if given[i] < largest] or [i for i in range(1, amount) if given[i] < limit]
        pool, remaining = sum([weights[i] for i in movable]), surplus
        for i in movable:
            addition = min(limit - given[i], max(1, remaining * weights[i] // pool), surplus)
            given[i] = given[i] + addition
            surplus = surplus - addition
    return np.array(given)


def gaussian(stream_key, dims, spread, limit, pieces=(), kind=jnp.bfloat16):
    entries = jax.random.normal(stream_key, dims, jnp.float32) * spread
    if len(pieces) > 0:
        entries = levels(stream_key, dims, pieces, -0.22, 0.18) * entries
    return jnp.clip(entries, min=-limit, max=limit).astype(kind)


def setup_inputs(seed: int = 0) -> dict:
    seeds = jax.random.split(jax.random.key(seed), 8)
    tokens = gaussian(seeds[0], (TOKENS, D), 1.0, 6.0, ((0, 4), (1, 8)))
    out_grad = gaussian(seeds[1], (TOKENS, D), 0.25, 1.5, ((0, 4), (1, 8)))
    probs = jnp.clip(0.1 + 0.9 * jax.random.uniform(seeds[2], (TOKENS, TOP), jnp.float32) ** levels(seeds[2], (TOKENS, TOP), ((0, 4),), -0.2, 0.2), 0.1, 1.0)
    expert_ids_keys = jax.random.split(jax.random.fold_in(seeds[3], 1), TOKENS // TOK_CTX)
    expert_ids_turns = jax.random.permutation(jax.random.fold_in(seeds[3], 3), TOKENS // TOK_CTX)
    expert_ids = jax.vmap(lambda own, number: shared_out(jax.random.fold_in(seeds[3], 2), own, number, TOK_CTX, EXPERTS, TOP, CAP, 2))(expert_ids_keys, expert_ids_turns).reshape((TOKENS, TOP))
    w_gate = gaussian(seeds[4], (EWIN, D, HID), D ** -0.5, 0.09375, ((0, 8), (1, 4)))
    w_up = gaussian(seeds[5], (EWIN, D, HID), D ** -0.5, 0.09375, ((0, 8), (1, 4)))
    w_down = gaussian(seeds[6], (EWIN, HID, D), HID ** -0.5, 0.1875, ((0, 8), (2, 4)))
    return {"tokens": tokens, "out_grad": out_grad, "probs": probs, "expert_ids": expert_ids, "w_gate": w_gate, "w_up": w_up, "w_down": w_down}


def reference(tokens, out_grad, probs, expert_ids, w_gate, w_up, w_down):
    blocks = TOKENS // TOK_CTX
    slot_rows = blocks * CAP
    pick_count = TOK_CTX * TOP
    chosen_ids = expert_ids.reshape(blocks, pick_count)
    weights = probs.reshape(blocks, pick_count)
    token_index = (jnp.arange(blocks, dtype=jnp.int32)[:, None] * TOK_CTX
                   + jnp.arange(pick_count, dtype=jnp.int32)[None, :] // TOP)
    block_base = jnp.arange(blocks, dtype=jnp.int32)[:, None] * CAP

    def per_expert(running, expert):
        chosen = (chosen_ids == expert).astype(jnp.int32)
        ranking = jnp.cumsum(chosen, axis=1) - chosen
        target = jnp.where(chosen > 0, block_base + ranking, slot_rows).reshape(-1).astype(jnp.int32)
        token_table = jnp.zeros((slot_rows,), jnp.int32).at[target].set(token_index.reshape(-1), mode="drop")
        slot_weight = jnp.zeros((slot_rows,), jnp.float32).at[target].set(weights.reshape(-1), mode="drop")
        filled = jnp.zeros((slot_rows,), jnp.int32).at[target].set(1, mode="drop")
        occupied = (filled > 0)[:, None]
        slot_tokens = jnp.where(occupied, tokens[token_table], jnp.zeros((), tokens.dtype))
        slot_grads = jnp.where(occupied, out_grad[token_table], jnp.zeros((), out_grad.dtype))
        gate_local = w_gate[expert]
        up_local = w_up[expert]
        down_local = w_down[expert]
        gate_sum = jnp.dot(slot_tokens, gate_local, preferred_element_type=jnp.float32)
        up_sum = jnp.dot(slot_tokens, up_local, preferred_element_type=jnp.float32)
        back_sum = jnp.dot(slot_grads, down_local.T, preferred_element_type=jnp.float32)
        weight_col = slot_weight[:, None]
        sigmoid_gate = jax.nn.sigmoid(gate_sum)
        silu_gate = gate_sum * sigmoid_gate
        hidden_grad = weight_col * back_sum
        hidden_weighted = (weight_col * silu_gate * up_sum).astype(jnp.bfloat16)
        up_grad = (hidden_grad * silu_gate).astype(jnp.bfloat16)
        gate_grad = (hidden_grad * up_sum * sigmoid_gate * (1.0 + gate_sum * (1.0 - sigmoid_gate))).astype(jnp.bfloat16)
        slot_grad = (jnp.dot(gate_grad, gate_local.T, preferred_element_type=jnp.float32)
                     + jnp.dot(up_grad, up_local.T, preferred_element_type=jnp.float32)).astype(jnp.bfloat16)
        running = running.at[token_table].add(jnp.where(occupied, slot_grad.astype(jnp.float32), 0.0))
        grad_gate = jnp.dot(slot_tokens.T, gate_grad, preferred_element_type=jnp.float32).astype(jnp.bfloat16)
        grad_up = jnp.dot(slot_tokens.T, up_grad, preferred_element_type=jnp.float32).astype(jnp.bfloat16)
        grad_down = jnp.dot(hidden_weighted.T, slot_grads, preferred_element_type=jnp.float32).astype(jnp.bfloat16)
        return running, (grad_gate, grad_up, grad_down)

    running, grads = lax.scan(per_expert, jnp.zeros((TOKENS, D), jnp.float32), jnp.arange(EWIN, dtype=jnp.int32))
    return running.astype(jnp.bfloat16), grads[0], grads[1], grads[2]
```

```python
import functools

import jax
import jax.numpy as jnp
from jax import lax
from jax.experimental import pallas as pl
from jax.experimental.pallas import tpu as pltpu
from jax.sharding import PartitionSpec as P

CAP = 16
MESH = pl.DeviceIdType.MESH
SUM_TYPE = jnp.float32
CONTRACT_FIRST = (((0,), (0,)), ((), ()))
CONTRACT_LAST = (((1,), (1,)), ((), ()))


def dot_f32(a, b, dims=(((1,), (0,)), ((), ()))):
    return lax.dot_general(a, b, dims, preferred_element_type=jnp.float32)


def remote(src, dst, send_sem, recv_sem, device):
    return pltpu.make_async_remote_copy(
        src_ref=src,
        dst_ref=dst,
        send_sem=send_sem,
        recv_sem=recv_sem,
        device_id=device,
        device_id_type=MESH,
    )


def steps(count, body):
    if count <= 8:
        for k in range(count):
            body(k)
    else:
        lax.fori_loop(0, count, lambda k, c: (body(k), c)[1], 0)


def exchange_kernel(
    ep,
    edp,
    tok_ref,
    grad_ref,
    probs_ref,
    ids_ref,
    wg_hbm,
    wu_hbm,
    wd_hbm,
    disp_out,
    ret_out,
    x_out,
    y_out,
    gg_out,
    ug_out,
    hw_out,
    wg,
    wu,
    wd,
    disp_t,
    pick_w,
    send_t,
    send_y,
    recv_t,
    recv_y,
    part,
    send_p,
    recv_p,
    hid,
    send_s,
    ret,
    w_sem,
    ss_t,
    rs_t,
    ss_y,
    rs_y,
    ss_p,
    rs_p,
    ss_h,
    rs_h,
    ss_r,
    rs_r,
):
    me_i = lax.axis_index("ep")
    me_j = lax.axis_index("edp")
    per = edp // ep
    home = me_j // per
    my_part = lax.rem(me_j, per)
    tok_rows, feat = tok_ref.shape
    slots = edp * CAP
    mine = pl.ds(pl.multiple_of(me_i * CAP, CAP), CAP)
    at_home = home == me_i

    loads = [
        pltpu.make_async_copy(src.at[0], dst, w_sem.at[n])
        for n, (src, dst) in enumerate(((wg_hbm, wg), (wu_hbm, wu), (wd_hbm, wd)))
    ]
    for load in loads:
        load.start()

    barrier = pltpu.get_barrier_semaphore()

    def greet(device):
        pl.semaphore_signal(barrier, inc=1, device_id=device, device_id_type=MESH)

    def greet_experts(k):
        e = lax.rem(me_j + 1 + k, edp)

        @pl.when(jnp.logical_not(jnp.logical_and(at_home, e == me_j)))
        def _():
            greet((home, e))

    def greet_owners(k):
        i = lax.rem(me_i + k // per, ep)
        j = me_i * per + lax.rem(k, per)

        @pl.when(jnp.logical_not(jnp.logical_and(i == me_i, j == me_j)))
        def _():
            greet((i, j))

    steps(edp, greet_experts)
    steps(edp, greet_owners)
    for d in range(1, ep):
        greet((lax.rem(me_i + d, ep), me_j))

    lane = lax.broadcasted_iota(jnp.int32, (tok_rows, slots), 1)
    expert = lax.shift_right_logical(lane, 4)
    place = lax.bitwise_and(lane, CAP - 1).astype(jnp.float32)
    chosen = jnp.zeros((tok_rows, slots), jnp.float32)
    weight = jnp.zeros((tok_rows, slots), jnp.float32)
    for k in range(ids_ref.shape[1]):
        hit = ids_ref[:, k : k + 1] == expert
        chosen = jnp.where(hit, 1.0, chosen)
        weight = jnp.where(hit, probs_ref[:, k : k + 1], weight)
    row = lax.broadcasted_iota(jnp.int32, (tok_rows, tok_rows), 0)
    col = lax.broadcasted_iota(jnp.int32, (tok_rows, tok_rows), 1)
    before = jnp.where(col < row, 1.0, 0.0).astype(jnp.bfloat16)
    rank = dot_f32(before, chosen.astype(jnp.bfloat16))
    disp = jnp.where(rank == place, chosen, 0.0)
    disp_out[...] = disp.astype(jnp.bfloat16)
    disp_t[...] = disp.T.astype(jnp.bfloat16)
    pick_w[...] = (disp * weight).T
    send_t[...] = dot_f32(disp_t[...], tok_ref[...]).astype(jnp.bfloat16)

    @pl.when(at_home)
    def _():
        pl.semaphore_wait(barrier, 2 * edp + ep - 1 - 2)

    @pl.when(jnp.logical_not(at_home))
    def _():
        pl.semaphore_wait(barrier, 2 * edp + ep - 1)

    def dispatch(k, send, recv, send_sem, recv_sem, action):
        e = lax.rem(me_j + 1 + k, edp)
        here = jnp.logical_and(at_home, e == me_j)
        src = send.at[pl.ds(pl.multiple_of(e * CAP, CAP), CAP), :]
        dst = recv.at[my_part, mine, :]
        arrive = recv_sem.at[my_part, me_i]

        @pl.when(here)
        def _():
            if action == "start":
                pltpu.make_async_copy(src, dst, arrive).start()

        @pl.when(jnp.logical_not(here))
        def _():
            copy = remote(src, dst, send_sem.at[e], arrive, (home, e))
            if action == "start":
                copy.start()
            else:
                copy.wait_send()

    def landed(k, recv, recv_sem):
        i = k // per
        p = lax.rem(k, per)
        spot = recv.at[p, pl.ds(pl.multiple_of(i * CAP, CAP), CAP), :]
        pltpu.make_async_copy(spot, spot, recv_sem.at[p, i]).wait()

    steps(edp, lambda k: dispatch(k, send_t, recv_t, ss_t, rs_t, "start"))
    send_y[...] = dot_f32(disp_t[...], grad_ref[...]).astype(jnp.bfloat16)
    steps(edp, lambda k: dispatch(k, send_y, recv_y, ss_y, rs_y, "start"))

    def share_sum(m, total):
        part[m, :, :] = total
        if send_p is not part:
            send_p[m, :, :] = total.astype(SUM_TYPE)
        for d in range(1, ep):
            sum_copy(m, d).start()

    def sum_copy(m, d):
        to = lax.rem(me_i + d, ep)
        src = send_p.at[m, pl.ds(pl.multiple_of(to * CAP, CAP), CAP), :]
        return remote(
            src, recv_p.at[m, d - 1], ss_p.at[m, d - 1], rs_p.at[m, d - 1], (to, me_j)
        )

    def gathered_sum(m):
        total = part[m, mine, :]
        for d in range(1, ep):
            sum_copy(m, d).wait_recv()
            total = total + recv_p[m, d - 1, :, :].astype(jnp.float32)
        return total

    loads[0].wait()
    steps(edp, lambda k: landed(k, recv_t, rs_t))
    for p in range(per):
        x_out[:, p * feat : (p + 1) * feat] = recv_t[p, :, :]
    share_sum(0, dot_f32(x_out[...], wg[...]))
    loads[1].wait()
    share_sum(1, dot_f32(x_out[...], wu[...]))
    loads[2].wait()
    steps(edp, lambda k: landed(k, recv_y, rs_y))
    for p in range(per):
        y_out[:, p * feat : (p + 1) * feat] = recv_y[p, :, :]
    share_sum(2, dot_f32(y_out[...], wd[...], CONTRACT_LAST))

    own = pl.ds(pl.multiple_of(me_j * CAP, CAP), CAP)
    weight_col = jnp.sum(pick_w[own, :], axis=1, keepdims=True)

    def hid_copy(m, d):
        spot = hid.at[m, mine, :]
        return remote(
            spot, spot, ss_h.at[m, d - 1], rs_h.at[m, d - 1], (lax.rem(me_i + d, ep), me_j)
        )

    def hid_arrived(m):
        for d in range(1, ep):
            came = lax.rem(me_i + ep - d, ep)
            spot = hid.at[m, pl.ds(pl.multiple_of(came * CAP, CAP), CAP), :]
            pltpu.make_async_copy(spot, spot, rs_h.at[m, d - 1]).wait()

    def share_hidden(m, value):
        hid[m, mine, :] = value.astype(jnp.bfloat16)
        for d in range(1, ep):
            hid_copy(m, d).start()

    gate_sum = gathered_sum(0)
    up_sum = gathered_sum(1)
    sig = jax.nn.sigmoid(gate_sum)
    silu = gate_sum * sig
    slope = up_sum * sig * (1.0 + gate_sum * (1.0 - sig))
    hidden_grad = weight_col * gathered_sum(2)
    share_hidden(0, hidden_grad * slope)
    share_hidden(1, hidden_grad * silu)
    share_hidden(2, weight_col * silu * up_sum)

    hid_arrived(0)
    slot_grad = dot_f32(hid[0, :, :], wg[...], CONTRACT_LAST)
    hid_arrived(1)
    slot_grad = (slot_grad + dot_f32(hid[1, :, :], wu[...], CONTRACT_LAST)).astype(jnp.bfloat16)
    for p in range(per):
        send_s[p, :, :] = slot_grad[:, p * feat : (p + 1) * feat]

    def give_back(k, action):
        i = lax.rem(me_i + 1 + k // per, ep)
        p = lax.rem(k, per)
        j = me_i * per + p
        here = jnp.logical_and(i == me_i, j == me_j)
        src = send_s.at[p, pl.ds(pl.multiple_of(i * CAP, CAP), CAP), :]
        dst = ret.at[own, :]

        @pl.when(here)
        def _():
            if action == "start":
                pltpu.make_async_copy(src, dst, rs_r.at[me_j]).start()

        @pl.when(jnp.logical_not(here))
        def _():
            copy = remote(src, dst, ss_r.at[p, i], rs_r.at[me_j], (i, j))
            if action == "start":
                copy.start()
            else:
                copy.wait_send()

    def returned(e):
        spot = ret.at[pl.ds(pl.multiple_of(e * CAP, CAP), CAP), :]
        pltpu.make_async_copy(spot, spot, rs_r.at[e]).wait()

    steps(edp, lambda k: give_back(k, "start"))
    gg_out[...] = hid[0, :, :]
    ug_out[...] = hid[1, :, :]
    hid_arrived(2)
    hw_out[...] = hid[2, :, :]
    steps(edp, lambda k: dispatch(k, send_t, recv_t, ss_t, rs_t, "wait"))
    steps(edp, lambda k: dispatch(k, send_y, recv_y, ss_y, rs_y, "wait"))
    for m in range(3):
        for d in range(1, ep):
            sum_copy(m, d).wait_send()
            hid_copy(m, d).wait_send()
    steps(edp, returned)
    ret_out[...] = ret[...]
    steps(edp, lambda k: give_back(k, "wait"))


def grads_kernel(
    disp_ref, ret_ref, x_ref, y_ref, gg_ref, ug_ref, hw_ref, tg_ref, dg_ref, du_ref, dd_ref
):
    dg_ref[0, :, :] = dot_f32(x_ref[...], gg_ref[...], CONTRACT_FIRST).astype(jnp.bfloat16)
    du_ref[0, :, :] = dot_f32(x_ref[...], ug_ref[...], CONTRACT_FIRST).astype(jnp.bfloat16)
    dd_ref[0, :, :] = dot_f32(hw_ref[...], y_ref[...], CONTRACT_FIRST).astype(jnp.bfloat16)
    tg_ref[...] = dot_f32(disp_ref[...], ret_ref[...]).astype(jnp.bfloat16)


def per_device(tokens, out_grad, probs, expert_ids, w_gate, w_up, w_down):
    ep, edp = lax.axis_size("ep"), lax.axis_size("edp")
    per = edp // ep
    tok_rows, feat = tokens.shape
    width, hidden = w_gate.shape[1:]
    slots = edp * CAP
    rows = ep * CAP
    bf16, f32 = jnp.bfloat16, jnp.float32
    vmem = pl.BlockSpec(memory_space=pltpu.VMEM)
    anywhere = pl.BlockSpec(memory_space=pl.ANY)
    dma = pltpu.SemaphoreType.DMA
    disp, ret, x_s, y_s, gg, ug, hw = pl.pallas_call(
        functools.partial(exchange_kernel, ep, edp),
        out_shape=[
            jax.ShapeDtypeStruct((tok_rows, slots), bf16),
            jax.ShapeDtypeStruct((slots, feat), bf16),
            jax.ShapeDtypeStruct((rows, width), bf16),
            jax.ShapeDtypeStruct((rows, width), bf16),
            jax.ShapeDtypeStruct((rows, hidden), bf16),
            jax.ShapeDtypeStruct((rows, hidden), bf16),
            jax.ShapeDtypeStruct((rows, hidden), bf16),
        ],
        in_specs=[vmem] * 4 + [anywhere] * 3,
        out_specs=[vmem] * 7,
        scratch_shapes=[
            pltpu.VMEM((width, hidden), bf16),
            pltpu.VMEM((width, hidden), bf16),
            pltpu.VMEM((hidden, width), bf16),
            pltpu.VMEM((slots, tok_rows), bf16),
            pltpu.VMEM((slots, tok_rows), f32),
            pltpu.VMEM((slots, feat), bf16),
            pltpu.VMEM((slots, feat), bf16),
            pltpu.VMEM((per, rows, feat), bf16),
            pltpu.VMEM((per, rows, feat), bf16),
            pltpu.VMEM((3, rows, hidden), f32),
            pltpu.VMEM((3, rows, hidden), SUM_TYPE),
            pltpu.VMEM((3, ep - 1, CAP, hidden), SUM_TYPE),
            pltpu.VMEM((3, rows, hidden), bf16),
            pltpu.VMEM((per, rows, feat), bf16),
            pltpu.VMEM((slots, feat), bf16),
            dma((3,)),
            dma((edp,)),
            dma((per, ep)),
            dma((edp,)),
            dma((per, ep)),
            dma((3, ep - 1)),
            dma((3, ep - 1)),
            dma((3, ep - 1)),
            dma((3, ep - 1)),
            dma((per, ep)),
            dma((edp,)),
        ],
        compiler_params=pltpu.CompilerParams(
            collective_id=0, has_side_effects=True, vmem_limit_bytes=48 * 1024 * 1024
        ),
        cost_estimate=pl.CostEstimate(
            flops=10 * rows * width * hidden,
            bytes_accessed=6 * width * hidden,
            transcendentals=CAP * hidden,
        ),
    )(tokens, out_grad, probs, expert_ids, w_gate, w_up, w_down)

    tiles = max(1, min(4, width // 128))

    def whole(shape):
        return pl.BlockSpec(shape, lambda n: (0, 0))

    token_grad, grad_gate, grad_up, grad_down = pl.pallas_call(
        grads_kernel,
        grid=(tiles,),
        out_shape=[
            jax.ShapeDtypeStruct((tok_rows, feat), bf16),
            jax.ShapeDtypeStruct((1, width, hidden), bf16),
            jax.ShapeDtypeStruct((1, width, hidden), bf16),
            jax.ShapeDtypeStruct((1, hidden, width), bf16),
        ],
        in_specs=[
            pl.BlockSpec((tok_rows // tiles, slots), lambda n: (n, 0)),
            whole((slots, feat)),
            pl.BlockSpec((rows, width // tiles), lambda n: (0, n)),
            whole((rows, width)),
            whole((rows, hidden)),
            whole((rows, hidden)),
            pl.BlockSpec((rows, hidden // tiles), lambda n: (0, n)),
        ],
        out_specs=[
            pl.BlockSpec((tok_rows // tiles, feat), lambda n: (n, 0)),
            pl.BlockSpec((1, width // tiles, hidden), lambda n: (0, n, 0)),
            pl.BlockSpec((1, width // tiles, hidden), lambda n: (0, n, 0)),
            pl.BlockSpec((1, hidden // tiles, width), lambda n: (0, n, 0)),
        ],
        compiler_params=pltpu.CompilerParams(vmem_limit_bytes=32 * 1024 * 1024),
        cost_estimate=pl.CostEstimate(
            flops=6 * rows * width * hidden,
            bytes_accessed=6 * width * hidden,
            transcendentals=0,
        ),
    )(disp, ret, x_s, y_s, gg, ug, hw)
    return token_grad, grad_gate, grad_up, grad_down


def solution(mesh):
    placed = (
        P("ep", "edp"),
        P("ep", "edp"),
        P("ep", None),
        P("ep", None),
        P("edp", "ep", None),
        P("edp", "ep", None),
        P("edp", None, "ep"),
    )
    return jax.shard_map(
        per_device,
        mesh=mesh,
        in_specs=placed,
        out_specs=(
            P("ep", "edp"),
            P("edp", "ep", None),
            P("edp", "ep", None),
            P("edp", None, "ep"),
        ),
        check_vma=False,
    )
```

```python
import functools

import jax
import jax.numpy as jnp
from jax import lax
from jax.experimental import pallas as pl
from jax.experimental.pallas import tpu as pltpu
from jax.sharding import PartitionSpec as P

CAP = 16
MESH = pl.DeviceIdType.MESH
SUM_TYPE = jnp.bfloat16
CONTRACT_FIRST = (((0,), (0,)), ((), ()))
CONTRACT_LAST = (((1,), (1,)), ((), ()))


def dot_f32(a, b, dims=(((1,), (0,)), ((), ()))):
    return lax.dot_general(a, b, dims, preferred_element_type=jnp.float32)


def remote(src, dst, send_sem, recv_sem, device):
    return pltpu.make_async_remote_copy(
        src_ref=src,
        dst_ref=dst,
        send_sem=send_sem,
        recv_sem=recv_sem,
        device_id=device,
        device_id_type=MESH,
    )


def steps(count, body):
    if count <= 8:
        for k in range(count):
            body(k)
    else:
        lax.fori_loop(0, count, lambda k, c: (body(k), c)[1], 0)


def exchange_kernel(
    ep,
    edp,
    tok_hbm,
    grad_hbm,
    probs_hbm,
    ids_hbm,
    wg_hbm,
    wu_hbm,
    wd_hbm,
    disp_out,
    ret_out,
    x_out,
    y_out,
    gg_out,
    ug_out,
    hw_out,
    wg,
    wu,
    wd,
    tok_ref,
    grad_ref,
    probs_ref,
    ids_ref,
    pick_w,
    send_t,
    send_y,
    mid_t,
    mid_y,
    recv_t,
    recv_y,
    part,
    send_p,
    recv_p,
    hid,
    send_s,
    ret,
    w_sem,
    ss_t,
    rs_t,
    ss_y,
    rs_y,
    ss_tb,
    rs_tb,
    ss_yb,
    rs_yb,
    ss_p,
    rs_p,
    ss_h,
    rs_h,
    ss_r,
    rs_r,
):
    me_i = lax.axis_index("ep")
    me_j = lax.axis_index("edp")
    per = edp // ep
    home = me_j // per
    tok_rows, feat = tok_ref.shape
    slots = edp * CAP
    mine = pl.ds(pl.multiple_of(me_i * CAP, CAP), CAP)
    at_home = home == me_i

    sources = (ids_hbm, probs_hbm, tok_hbm, grad_hbm, wg_hbm.at[0], wu_hbm.at[0], wd_hbm.at[0])
    places = (ids_ref, probs_ref, tok_ref, grad_ref, wg, wu, wd)
    loads = [
        pltpu.make_async_copy(src, dst, w_sem.at[n])
        for n, (src, dst) in enumerate(zip(sources, places))
    ]
    for load in loads:
        load.start()

    barrier = pltpu.get_barrier_semaphore()

    def greet(device):
        pl.semaphore_signal(barrier, inc=1, device_id=device, device_id_type=MESH)

    def greet_experts(k):
        e = lax.rem(me_j + 1 + k, edp)

        @pl.when(jnp.logical_not(jnp.logical_and(at_home, e == me_j)))
        def _():
            greet((home, e))

    def greet_owners(k):
        i = lax.rem(me_i + k // per, ep)
        j = me_i * per + lax.rem(k, per)

        @pl.when(jnp.logical_not(jnp.logical_and(i == me_i, j == me_j)))
        def _():
            greet((i, j))

    steps(edp, greet_experts)
    steps(edp, greet_owners)
    for d in range(1, edp):
        greet((me_i, lax.rem(me_j + d, edp)))
    for d in range(1, ep):
        greet((lax.rem(me_i + d, ep), me_j))

    slot = lax.broadcasted_iota(jnp.int32, (slots, tok_rows), 0)
    expert = lax.shift_right_logical(slot, 4)
    place = lax.bitwise_and(slot, CAP - 1).astype(jnp.float32)
    chosen = jnp.zeros((slots, tok_rows), jnp.float32)
    weight = jnp.zeros((slots, tok_rows), jnp.float32)
    loads[0].wait()
    loads[1].wait()
    for k in range(ids_ref.shape[0]):
        hit = ids_ref[k : k + 1, :] == expert
        chosen = jnp.where(hit, 1.0, chosen)
        weight = jnp.where(hit, probs_ref[k : k + 1, :], weight)
    row = lax.broadcasted_iota(jnp.int32, (tok_rows, tok_rows), 0)
    col = lax.broadcasted_iota(jnp.int32, (tok_rows, tok_rows), 1)
    before = jnp.where(row < col, 1.0, 0.0).astype(jnp.bfloat16)
    rank = dot_f32(chosen.astype(jnp.bfloat16), before)
    disp = jnp.where(rank == place, chosen, 0.0)
    disp_out[...] = disp.astype(jnp.bfloat16)
    pick_w[...] = disp * weight
    loads[2].wait()
    send_t[...] = dot_f32(disp_out[...], tok_ref[...]).astype(jnp.bfloat16)

    @pl.when(at_home)
    def _():
        pl.semaphore_wait(barrier, 3 * edp - 1 + ep - 1 - 2)

    @pl.when(jnp.logical_not(at_home))
    def _():
        pl.semaphore_wait(barrier, 3 * edp - 1 + ep - 1)

    def rows_of(first, count):
        return pl.ds(pl.multiple_of(first * CAP, CAP), count * CAP)

    def along_experts(d, send, mid, send_sem, recv_sem):
        e = lax.rem(me_j + d, edp)
        return remote(
            send.at[rows_of(e, 1), :],
            mid.at[rows_of(me_j, 1), :],
            send_sem.at[d - 1],
            recv_sem.at[d - 1],
            (me_i, e),
        )

    def start_experts(send, mid, send_sem, recv_sem):
        steps(edp - 1, lambda k: along_experts(k + 1, send, mid, send_sem, recv_sem).start())
        mid[rows_of(me_j, 1), :] = send[rows_of(me_j, 1), :]

    def along_blocks(d, mid, recv, send_sem, recv_sem):
        to = lax.rem(me_i + d, ep)
        return remote(
            mid.at[rows_of(to * per, per), :],
            recv.at[me_i],
            send_sem.at[d - 1],
            recv_sem.at[d - 1],
            (to, me_j),
        )

    def came_from(i, mid, recv_sem):
        for p in range(per):
            j = i * per + p
            spot = mid.at[rows_of(j, 1), :]

            @pl.when(j != me_j)
            def _():
                n = lax.rem(me_j - j + edp, edp) - 1
                pltpu.make_async_copy(spot, spot, recv_sem.at[n]).wait()

    def forward(mid, recv, mid_sem, send_sem, recv_sem):
        for d in range(1, ep):
            came_from(lax.rem(me_i + d, ep), mid, mid_sem)
            along_blocks(d, mid, recv, send_sem, recv_sem).start()
        came_from(me_i, mid, mid_sem)
        recv[me_i, :, :] = mid[rows_of(me_i * per, per), :]

    def assemble(out, mid, recv, send_sem, recv_sem):
        for d in range(1, ep):
            along_blocks(d, mid, recv, send_sem, recv_sem).wait_recv()
        for i in range(ep):
            for p in range(per):
                out[i * CAP : (i + 1) * CAP, p * feat : (p + 1) * feat] = recv[
                    i, p * CAP : (p + 1) * CAP, :
                ]

    start_experts(send_t, mid_t, ss_t, rs_t)
    loads[3].wait()
    send_y[...] = dot_f32(disp_out[...], grad_ref[...]).astype(jnp.bfloat16)
    start_experts(send_y, mid_y, ss_y, rs_y)
    forward(mid_t, recv_t, rs_t, ss_tb, rs_tb)

    def share_sum(m, total):
        send_p[m, :, :] = total.astype(SUM_TYPE)
        for d in range(1, ep):
            sum_copy(m, d).start()
        part[m, :, :] = total

    def sum_copy(m, d):
        to = lax.rem(me_i + d, ep)
        src = send_p.at[m, pl.ds(pl.multiple_of(to * CAP, CAP), CAP), :]
        return remote(
            src, recv_p.at[m, d - 1], ss_p.at[m, d - 1], rs_p.at[m, d - 1], (to, me_j)
        )

    def gathered_sum(m):
        total = part[m, mine, :]
        for d in range(1, ep):
            sum_copy(m, d).wait_recv()
            total = total + recv_p[m, d - 1, :, :].astype(jnp.float32)
        return total

    loads[4].wait()
    assemble(x_out, mid_t, recv_t, ss_tb, rs_tb)
    share_sum(0, dot_f32(x_out[...], wg[...]))
    forward(mid_y, recv_y, rs_y, ss_yb, rs_yb)
    loads[5].wait()
    share_sum(1, dot_f32(x_out[...], wu[...]))
    loads[6].wait()
    assemble(y_out, mid_y, recv_y, ss_yb, rs_yb)
    share_sum(2, dot_f32(y_out[...], wd[...], CONTRACT_LAST))

    own = pl.ds(pl.multiple_of(me_j * CAP, CAP), CAP)
    weight_col = jnp.sum(pick_w[own, :], axis=1, keepdims=True)

    def hid_copy(m, d):
        spot = hid.at[m, mine, :]
        return remote(
            spot, spot, ss_h.at[m, d - 1], rs_h.at[m, d - 1], (lax.rem(me_i + d, ep), me_j)
        )

    def hid_arrived(m):
        for d in range(1, ep):
            came = lax.rem(me_i + ep - d, ep)
            spot = hid.at[m, pl.ds(pl.multiple_of(came * CAP, CAP), CAP), :]
            pltpu.make_async_copy(spot, spot, rs_h.at[m, d - 1]).wait()

    def share_hidden(m, value):
        hid[m, mine, :] = value.astype(jnp.bfloat16)
        for d in range(1, ep):
            hid_copy(m, d).start()

    gate_sum = gathered_sum(0)
    up_sum = gathered_sum(1)
    sig = jax.nn.sigmoid(gate_sum)
    silu = gate_sum * sig
    slope = up_sum * sig * (1.0 + gate_sum * (1.0 - sig))
    hidden_grad = weight_col * gathered_sum(2)
    share_hidden(0, hidden_grad * slope)
    share_hidden(1, hidden_grad * silu)
    share_hidden(2, weight_col * silu * up_sum)

    hid_arrived(0)
    slot_grad = dot_f32(hid[0, :, :], wg[...], CONTRACT_LAST)
    hid_arrived(1)
    slot_grad = (slot_grad + dot_f32(hid[1, :, :], wu[...], CONTRACT_LAST)).astype(jnp.bfloat16)
    for p in range(per):
        send_s[p, :, :] = slot_grad[:, p * feat : (p + 1) * feat]

    def give_back(k, action):
        i = lax.rem(me_i + 1 + k // per, ep)
        p = lax.rem(k, per)
        j = me_i * per + p
        here = jnp.logical_and(i == me_i, j == me_j)
        src = send_s.at[p, pl.ds(pl.multiple_of(i * CAP, CAP), CAP), :]
        dst = ret.at[own, :]

        @pl.when(here)
        def _():
            if action == "start":
                pltpu.make_async_copy(src, dst, rs_r.at[me_j]).start()

        @pl.when(jnp.logical_not(here))
        def _():
            copy = remote(src, dst, ss_r.at[p, i], rs_r.at[me_j], (i, j))
            if action == "start":
                copy.start()
            else:
                copy.wait_send()

    def returned(e):
        spot = ret.at[pl.ds(pl.multiple_of(e * CAP, CAP), CAP), :]
        pltpu.make_async_copy(spot, spot, rs_r.at[e]).wait()

    steps(edp, lambda k: give_back(k, "start"))
    gg_out[...] = hid[0, :, :]
    ug_out[...] = hid[1, :, :]
    hid_arrived(2)
    hw_out[...] = hid[2, :, :]
    for args in ((send_t, mid_t, ss_t, rs_t), (send_y, mid_y, ss_y, rs_y)):
        steps(edp - 1, lambda k: along_experts(k + 1, *args).wait_send())
    for args in ((mid_t, recv_t, ss_tb, rs_tb), (mid_y, recv_y, ss_yb, rs_yb)):
        for d in range(1, ep):
            along_blocks(d, *args).wait_send()
    for m in range(3):
        for d in range(1, ep):
            sum_copy(m, d).wait_send()
            hid_copy(m, d).wait_send()
    steps(edp, returned)
    ret_out[...] = ret[...]
    steps(edp, lambda k: give_back(k, "wait"))


def grads_kernel(
    disp_ref, ret_ref, x_ref, y_ref, gg_ref, ug_ref, hw_ref, tg_ref, dg_ref, du_ref, dd_ref
):
    dg_ref[0, :, :] = dot_f32(x_ref[...], gg_ref[...], CONTRACT_FIRST).astype(jnp.bfloat16)
    du_ref[0, :, :] = dot_f32(x_ref[...], ug_ref[...], CONTRACT_FIRST).astype(jnp.bfloat16)
    dd_ref[0, :, :] = dot_f32(hw_ref[...], y_ref[...], CONTRACT_FIRST).astype(jnp.bfloat16)

    @pl.when(pl.program_id(0) == 0)
    def _():
        tg_ref[...] = dot_f32(disp_ref[...], ret_ref[...], CONTRACT_FIRST).astype(jnp.bfloat16)


def per_device(tokens, out_grad, probs, expert_ids, w_gate, w_up, w_down):
    ep, edp = lax.axis_size("ep"), lax.axis_size("edp")
    per = edp // ep
    tok_rows, feat = tokens.shape
    picks = probs.shape[1]
    width, hidden = w_gate.shape[1:]
    slots = edp * CAP
    rows = ep * CAP
    bf16, f32 = jnp.bfloat16, jnp.float32
    vmem = pl.BlockSpec(memory_space=pltpu.VMEM)
    hbm = pl.BlockSpec(memory_space=pltpu.HBM)
    dma = pltpu.SemaphoreType.DMA
    disp, ret, x_s, y_s, gg, ug, hw = pl.pallas_call(
        functools.partial(exchange_kernel, ep, edp),
        out_shape=[
            jax.ShapeDtypeStruct((slots, tok_rows), bf16),
            jax.ShapeDtypeStruct((slots, feat), bf16),
            jax.ShapeDtypeStruct((rows, width), bf16),
            jax.ShapeDtypeStruct((rows, width), bf16),
            jax.ShapeDtypeStruct((rows, hidden), bf16),
            jax.ShapeDtypeStruct((rows, hidden), bf16),
            jax.ShapeDtypeStruct((rows, hidden), bf16),
        ],
        in_specs=[hbm] * 7,
        out_specs=[vmem] * 7,
        scratch_shapes=[
            pltpu.VMEM((width, hidden), bf16),
            pltpu.VMEM((width, hidden), bf16),
            pltpu.VMEM((hidden, width), bf16),
            pltpu.VMEM((tok_rows, feat), bf16),
            pltpu.VMEM((tok_rows, feat), bf16),
            pltpu.VMEM((picks, tok_rows), f32),
            pltpu.VMEM((picks, tok_rows), jnp.int32),
            pltpu.VMEM((slots, tok_rows), f32),
            pltpu.VMEM((slots, feat), bf16),
            pltpu.VMEM((slots, feat), bf16),
            pltpu.VMEM((slots, feat), bf16),
            pltpu.VMEM((slots, feat), bf16),
            pltpu.VMEM((ep, per * CAP, feat), bf16),
            pltpu.VMEM((ep, per * CAP, feat), bf16),
            pltpu.VMEM((3, rows, hidden), f32),
            pltpu.VMEM((3, rows, hidden), SUM_TYPE),
            pltpu.VMEM((3, ep - 1, CAP, hidden), SUM_TYPE),
            pltpu.VMEM((3, rows, hidden), bf16),
            pltpu.VMEM((per, rows, feat), bf16),
            pltpu.VMEM((slots, feat), bf16),
            dma((7,)),
            dma((edp - 1,)),
            dma((edp - 1,)),
            dma((edp - 1,)),
            dma((edp - 1,)),
            dma((ep - 1,)),
            dma((ep - 1,)),
            dma((ep - 1,)),
            dma((ep - 1,)),
            dma((3, ep - 1)),
            dma((3, ep - 1)),
            dma((3, ep - 1)),
            dma((3, ep - 1)),
            dma((per, ep)),
            dma((edp,)),
        ],
        compiler_params=pltpu.CompilerParams(
            collective_id=0, has_side_effects=True, vmem_limit_bytes=60 * 1024 * 1024
        ),
        cost_estimate=pl.CostEstimate(
            flops=10 * rows * width * hidden,
            bytes_accessed=6 * width * hidden,
            transcendentals=CAP * hidden,
        ),
    )(tokens, out_grad, probs.T, expert_ids.T, w_gate, w_up, w_down)

    tiles = max(1, min(4, width // 128))

    def whole(shape):
        return pl.BlockSpec(shape, lambda n: (0, 0))

    token_grad, grad_gate, grad_up, grad_down = pl.pallas_call(
        grads_kernel,
        grid=(tiles,),
        out_shape=[
            jax.ShapeDtypeStruct((tok_rows, feat), bf16),
            jax.ShapeDtypeStruct((1, width, hidden), bf16),
            jax.ShapeDtypeStruct((1, width, hidden), bf16),
            jax.ShapeDtypeStruct((1, hidden, width), bf16),
        ],
        in_specs=[
            whole((slots, tok_rows)),
            whole((slots, feat)),
            pl.BlockSpec((rows, width // tiles), lambda n: (0, n)),
            whole((rows, width)),
            whole((rows, hidden)),
            whole((rows, hidden)),
            pl.BlockSpec((rows, hidden // tiles), lambda n: (0, n)),
        ],
        out_specs=[
            whole((tok_rows, feat)),
            pl.BlockSpec((1, width // tiles, hidden), lambda n: (0, n, 0)),
            pl.BlockSpec((1, width // tiles, hidden), lambda n: (0, n, 0)),
            pl.BlockSpec((1, hidden // tiles, width), lambda n: (0, n, 0)),
        ],
        compiler_params=pltpu.CompilerParams(vmem_limit_bytes=60 * 1024 * 1024),
        cost_estimate=pl.CostEstimate(
            flops=6 * rows * width * hidden,
            bytes_accessed=6 * width * hidden,
            transcendentals=0,
        ),
    )(disp, ret, x_s, y_s, gg, ug, hw)
    return token_grad, grad_gate, grad_up, grad_down


def solution(mesh):
    placed = (
        P("ep", "edp"),
        P("ep", "edp"),
        P("ep", None),
        P("ep", None),
        P("edp", "ep", None),
        P("edp", "ep", None),
        P("edp", None, "ep"),
    )
    return jax.shard_map(
        per_device,
        mesh=mesh,
        in_specs=placed,
        out_specs=(
            P("ep", "edp"),
            P("edp", "ep", None),
            P("edp", "ep", None),
            P("edp", None, "ep"),
        ),
        check_vma=False,
    )
```
